32 devices in a mesh: row: 8 (over y, x, core), col: 4 (over z).
Axes of the slice: x: 2, y: 2, z: 4, core: 2. Of those that a mesh axis runs over, the one named last changes fastest.
Arguments:
- x_tiles: float32 [64, 4096], P(('row', 'col')), may hold values from -6 to 6
- ham_tiles: float32 [2048, 4096], P(('row', 'col')), may hold values from -0.125 to 0.125
- tile_rows: int32 [2048], P(('row', 'col')), may hold values from 0 to 7, as said below
- tile_cols: int32 [2048], P(('row', 'col')), may hold values from 0 to 15, as said below
- tile_count: int32 [32], P(('row', 'col')), may hold values from 0 to 64, as said below
Outputs:
- product: float32 [64, 4096], P(('row', 'col'))
The draws below stay inside these ranges and needn't reach their ends.
Inputs may be any that keep to these rules, and one draw needn't show every extreme that they name: For device d, its first tile_count[d] slots hold distinct positions (tile_rows, tile_cols) whose global tile row is at most the global tile column; the other slots are padding with indices in range. `tile_cols`: see tile_rows. `tile_count`: at most 64; equal to 64 on every device of row index 0.
All inputs are finite; a program needn't handle non-finite values.
Results may differ from the reference program's by a relative error of at most 0.0003.
Values sent between devices are 32-bit elements; how exact they have to be, the bound alone decides.
A program may use at most 128 MiB of HBM per device.

```python
import jax
import jax.numpy as jnp
from jax import lax

TILE = 64
VECS = 64
TPD = 2
NT = 64
MAXT = 64
N_ROW = 8
N_COL = 4
DEVICES = 32


def tile_layout(key):
    rows_blk = N_COL * TPD
    cols_blk = N_ROW * TPD
    positions = rows_blk * cols_blk
    dev = jnp.arange(DEVICES, dtype=jnp.int32)
    rindex = dev // N_COL
    cindex = dev % N_COL
    spot = jnp.arange(positions, dtype=jnp.int32)
    local_a = spot // cols_blk
    local_b = spot % cols_blk
    grow = rindex[:, None] * rows_blk + local_a[None, :]
    gcol = ((local_b // TPD)[None, :] * N_COL + cindex[:, None]) * TPD + (local_b % TPD)[None, :]
    usable = (grow <= gcol).astype(jnp.int32)
    eligible = jnp.sum(usable, axis=1)
    keys = jax.random.split(jax.random.fold_in(key, 7), DEVICES)
    perms = jax.vmap(lambda k: jax.random.permutation(k, positions))(keys).astype(jnp.int32)
    usable_perm = jnp.take_along_axis(usable, perms, axis=1)
    order = jnp.argsort(1 - usable_perm, axis=1, stable=True)
    chosen = jnp.take_along_axis(perms, order, axis=1)[:, :MAXT]
    weights = jax.random.randint(jax.random.fold_in(key, 11), (DEVICES,), 768, 1025, dtype=jnp.int32)
    counts = jnp.minimum(MAXT, eligible * weights // 1024).astype(jnp.int32)
    return ((chosen // cols_blk).astype(jnp.int32), (chosen % cols_blk).astype(jnp.int32), counts)


def draw_tile_rows(key, part):
    rows, cols, counts = tile_layout(key)
    return rows.reshape(-1)


def draw_tile_cols(key, part):
    rows, cols, counts = tile_layout(key)
    return cols.reshape(-1)


def draw_tile_count(key, part):
    rows, cols, counts = tile_layout(key)
    return counts


def shard_levels(stream_key, shape, pieces, low, largest):
    gain, own = 1.0, jax.random.fold_in(stream_key, 6)
    for axis_at, parts in pieces:
        heights = jnp.exp(jax.random.uniform(jax.random.fold_in(own, axis_at), (parts,), jnp.float32, low / len(pieces), largest / len(pieces)))
        gain = gain * jnp.repeat(heights, shape[axis_at] // parts).reshape([-1 if axis == axis_at else 1 for axis in range(len(shape))])
    return gain


def scatter_about(own_key, shape, scale, bound, cuts=(), held_as=jnp.bfloat16):
    array = jax.random.normal(own_key, shape, jnp.float32) * scale
    if len(cuts) > 0:
        array = shard_levels(own_key, shape, cuts, -0.22, 0.18) * array
    return jnp.clip(array, min=-bound, max=bound).astype(held_as)


def setup_inputs(seed: int = 0) -> dict:
    streams_of = jax.random.split(jax.random.key(seed), 6)
    x_tiles = scatter_about(streams_of[0], (NT, TILE * VECS), 1.0, 6.0, ((0, 32),), jnp.float32)
    ham_tiles = scatter_about(streams_of[1], (DEVICES * MAXT, TILE * TILE), (TILE * NT // 2) ** -0.5, 0.125, ((0, 32),), jnp.float32)
    tile_rows = draw_tile_rows(jax.random.fold_in(streams_of[5], 71), 0)
    tile_cols = draw_tile_cols(jax.random.fold_in(streams_of[5], 71), 0)
    tile_count = draw_tile_count(jax.random.fold_in(streams_of[5], 71), 0)
    return dict(x_tiles=x_tiles, ham_tiles=ham_tiles, tile_rows=tile_rows, tile_cols=tile_cols, tile_count=tile_count)


def reference(x_tiles, ham_tiles, tile_rows, tile_cols, tile_count):
    slots = MAXT
    tiles_all = ham_tiles.reshape(DEVICES, slots, TILE, TILE)
    rows_all = tile_rows.reshape(DEVICES, slots)
    cols_all = tile_cols.reshape(DEVICES, slots)
    device_ids = jnp.arange(DEVICES, dtype=jnp.int32)

    def one_device(total, inputs):
        tiles, rows, cols, count, dev = inputs
        rindex = dev // N_COL
        cindex = dev % N_COL
        grow = (rindex * N_COL * TPD + rows).astype(jnp.int32)
        gcol = (((cols // TPD) * N_COL + cindex) * TPD + cols % TPD).astype(jnp.int32)
        live = (jnp.arange(slots) < count).astype(jnp.float32)
        far = x_tiles[gcol].reshape(slots, TILE, VECS)
        near = x_tiles[grow].reshape(slots, TILE, VECS)
        forward = jnp.einsum("sij,sjk->sik", tiles, far, precision=lax.Precision.HIGHEST)
        backward = jnp.einsum("sji,sjk->sik", tiles, near, precision=lax.Precision.HIGHEST)
        forward = forward.reshape(slots, TILE * VECS) * live[:, None]
        backward = backward.reshape(slots, TILE * VECS) * live[:, None]
        total = total.at[grow].add(forward)
        total = total.at[gcol].add(backward)
        return total, None

    start = jnp.zeros((NT, TILE * VECS), jnp.float32)
    total, _ = lax.scan(one_device, start, (tiles_all, rows_all, cols_all, tile_count, device_ids))
    return total
```

```python
import functools

import jax
import jax.numpy as jnp
from jax import lax
from jax.experimental import pallas as pl
from jax.experimental.pallas import tpu as pltpu
from jax.sharding import PartitionSpec as P

TILE = 64
VECS = 64
LANES = 128
MESH = pl.DeviceIdType.MESH
F32 = jnp.float32
BF16 = jnp.bfloat16


def parts(value):
    high = value.astype(BF16)
    low = (value - high.astype(F32)).astype(BF16)
    return high, low


def kernel(
    n_row, n_col, tpd, slots,
    count_ref, rows_ref, cols_ref, x_ref, ham_ref, out_ref,
    ham, rows, cols, placed, m_high, m_low, far, near, stage, weights, near_t,
    up_own, up_got, low_own, low_got, turned,
    local_sems, far_send, far_recv, near_send, near_recv,
    up_send, up_recv, low_send, low_recv,
):
    r, c = lax.axis_index("row"), lax.axis_index("col")
    a_tiles, b_tiles = n_col * tpd, n_row * tpd
    positions = a_tiles * b_tiles
    packed = TILE * VECS // LANES
    wide = tpd * LANES

    def row_peer(k):
        return (lax.rem(r + k, n_row), c)

    def col_peer(k):
        return (r, lax.rem(c + k, n_col))

    get_x = pltpu.make_async_copy(x_ref, far.at[0], local_sems.at[0])
    get_near = pltpu.make_async_copy(x_ref, near.at[0], local_sems.at[1])
    get_rows = pltpu.make_async_copy(rows_ref, rows, local_sems.at[2])
    get_cols = pltpu.make_async_copy(cols_ref, cols, local_sems.at[3])
    get_ham = pltpu.make_async_copy(ham_ref, ham, local_sems.at[4])
    for copy in (get_x, get_near, get_rows, get_cols, get_ham):
        copy.start()

    barrier = pltpu.get_barrier_semaphore()
    for k in range(1, n_row):
        pl.semaphore_signal(barrier, inc=1, device_id=row_peer(k), device_id_type=MESH)
    for k in range(1, n_col):
        pl.semaphore_signal(barrier, inc=1, device_id=col_peer(k), device_id_type=MESH)
    pl.semaphore_wait(barrier, n_row + n_col - 2)

    get_x.wait()
    near_copies = []
    for k in range(1, n_col):
        copy = pltpu.make_async_remote_copy(
            src_ref=far.at[0], dst_ref=near.at[k],
            send_sem=near_send.at[k], recv_sem=near_recv.at[k],
            device_id=col_peer(n_col - k), device_id_type=MESH,
        )
        copy.start()
        near_copies.append(copy)
    far_copies = []
    for k in range(1, n_row):
        copy = pltpu.make_async_remote_copy(
            src_ref=far.at[0], dst_ref=far.at[k],
            send_sem=far_send.at[k], recv_sem=far_recv.at[k],
            device_id=row_peer(n_row - k), device_id_type=MESH,
        )
        copy.start()
        far_copies.append(copy)

    get_rows.wait()
    get_cols.wait()
    at_row = rows[...] - c * tpd
    at_row = jnp.where(at_row < 0, at_row + a_tiles, at_row)
    at_col = cols[...] - r * tpd
    at_col = jnp.where(at_col < 0, at_col + b_tiles, at_col)
    slot = lax.broadcasted_iota(jnp.int32, (1, slots), 1)
    place = jnp.where(slot < count_ref[0], at_row * b_tiles + at_col, -1)
    place = jnp.concatenate([place, place], axis=1)
    spot = lax.broadcasted_iota(jnp.int32, (positions, 2 * slots), 0)
    picks = jnp.where(spot == place, 1.0, 0.0).astype(BF16)

    get_ham.wait()
    for p in range(0, packed, 2):
        high, low = parts(ham[:, p * LANES:(p + 2) * LANES])
        both = jnp.concatenate([high, low], axis=0)
        put = jnp.dot(picks, both, preferred_element_type=F32)
        placed[p * positions:(p + 1) * positions, :] = put[:, :LANES]
        placed[(p + 1) * positions:(p + 2) * positions, :] = put[:, LANES:]

    def unfold(a, carry):
        for b in range(b_tiles):
            tile = placed[pl.ds(a * b_tiles + b, packed, stride=positions), :]
            high, low = parts(tile)
            at = pl.ds(pl.multiple_of(a * packed, packed), packed)
            m_high[at, b * LANES:(b + 1) * LANES] = high
            m_low[at, b * LANES:(b + 1) * LANES] = low
        return carry

    lax.fori_loop(0, a_tiles, unfold, 0)

    lane = lax.broadcasted_iota(jnp.int32, (TILE, LANES), 1)
    left = lane < TILE

    get_near.wait()
    for k in range(n_col):
        if k:
            near_copies[k - 1].wait_recv()
        for t in range(tpd):
            near_t[(k * tpd + t) * packed:(k * tpd + t + 1) * packed, :] = near[
                k, pl.ds(t, packed, stride=tpd), :
            ]
    high, low = parts(near_t[...].T)
    x_both = jnp.concatenate([high, low], axis=0)
    low_copies = []
    for k in list(range(1, n_row)) + [0]:
        block = slice(k * wide, (k + 1) * wide)
        first = jnp.dot(x_both, m_high[:, block], preferred_element_type=F32)
        second = jnp.dot(high, m_low[:, block], preferred_element_type=F32)
        total = first[:LANES] + first[LANES:] + second
        for t in range(0, tpd, 2):
            even = total[:, t * LANES:(t + 1) * LANES]
            odd = total[:, (t + 1) * LANES:(t + 2) * LANES]
            one = even[:TILE] + pltpu.roll(even[TILE:], TILE, 1)
            two = pltpu.roll(odd[:TILE], TILE, 1) + odd[TILE:]
            low_own[k, :, t * TILE:(t + 2) * TILE] = jnp.where(left, one, two)
        if k:
            copy = pltpu.make_async_remote_copy(
                src_ref=low_own.at[k], dst_ref=low_got.at[k],
                send_sem=low_send.at[k], recv_sem=low_recv.at[k],
                device_id=row_peer(k), device_id_type=MESH,
            )
            copy.start()
            low_copies.append(copy)

    half = left[:packed]
    for k in range(n_row):
        if k:
            far_copies[k - 1].wait_recv()
        for t in range(tpd):
            x = far[k, pl.ds(t, packed, stride=tpd), :]
            swapped = pltpu.roll(x, TILE, 1)
            stage[pl.ds(0, packed, stride=2), :] = jnp.where(half, x, 0.0)
            stage[pl.ds(1, packed, stride=2), :] = jnp.where(half, swapped, 0.0)
            stage[pl.ds(TILE, packed, stride=2), :] = jnp.where(half, 0.0, swapped)
            stage[pl.ds(TILE + 1, packed, stride=2), :] = jnp.where(half, 0.0, x)
            high, low = parts(stage[...])
            at = slice((k * tpd + t) * LANES, (k * tpd + t + 1) * LANES)
            weights[at, :LANES] = high
            weights[at, LANES:] = low
    first = jnp.dot(m_high[...], weights[...], preferred_element_type=F32)
    second = jnp.dot(m_low[...], weights[:, :LANES], preferred_element_type=F32)
    up_own[...] = first[:, :LANES] + first[:, LANES:] + second
    up_copies = []
    height = tpd * packed
    for k in range(1, n_col):
        copy = pltpu.make_async_remote_copy(
            src_ref=up_own.at[pl.ds(k * height, height)], dst_ref=up_got.at[k],
            send_sem=up_send.at[k], recv_sem=up_recv.at[k],
            device_id=col_peer(k), device_id_type=MESH,
        )
        copy.start()
        up_copies.append(copy)

    lower = low_own[0]
    for k in range(1, n_row):
        low_copies[k - 1].wait_recv()
        lower += low_got[k]
    turned[...] = jnp.concatenate([lower, lower], axis=0).T
    upper = up_own[:height, :]
    for k in range(1, n_col):
        up_copies[k - 1].wait_recv()
        upper += up_got[k]
    for t in range(tpd):
        even = turned[pl.ds(t * TILE, packed, stride=2), :]
        odd = turned[pl.ds(t * TILE + 1, packed, stride=2), :]
        out_ref[pl.ds(t, packed, stride=tpd), :] = (
            upper[t * packed:(t + 1) * packed] + jnp.where(half, even, odd)
        )
    for copy in near_copies + far_copies + low_copies + up_copies:
        copy.wait_send()


def solution(mesh):
    n_row, n_col = mesh.shape["row"], mesh.shape["col"]

    def shards(x_tiles, ham_tiles, tile_rows, tile_cols, tile_count):
        tpd, size = x_tiles.shape
        slots = ham_tiles.shape[0]
        packed = size // LANES
        a_tiles, b_tiles = n_col * tpd, n_row * tpd
        height = tpd * packed
        x = x_tiles.reshape(tpd, packed, LANES).transpose(1, 0, 2).reshape(height, LANES)
        anywhere = pl.BlockSpec(memory_space=pl.ANY)
        dma = pltpu.SemaphoreType.DMA
        out = pl.pallas_call(
            functools.partial(kernel, n_row, n_col, tpd, slots),
            out_shape=jax.ShapeDtypeStruct((height, LANES), F32),
            in_specs=[pl.BlockSpec(memory_space=pltpu.SMEM)] + [anywhere] * 4,
            out_specs=pl.BlockSpec(memory_space=pltpu.VMEM),
            scratch_shapes=[
                pltpu.VMEM((slots, size), F32),
                pltpu.VMEM((1, slots), jnp.int32),
                pltpu.VMEM((1, slots), jnp.int32),
                pltpu.VMEM((packed * a_tiles * b_tiles, LANES), F32),
                pltpu.VMEM((a_tiles * packed, b_tiles * LANES), BF16),
                pltpu.VMEM((a_tiles * packed, b_tiles * LANES), BF16),
                pltpu.VMEM((n_row, height, LANES), F32),
                pltpu.VMEM((n_col, height, LANES), F32),
                pltpu.VMEM((LANES, LANES), F32),
                pltpu.VMEM((b_tiles * LANES, 2 * LANES), BF16),
                pltpu.VMEM((a_tiles * packed, LANES), F32),
                pltpu.VMEM((a_tiles * packed, LANES), F32),
                pltpu.VMEM((n_col, height, LANES), F32),
                pltpu.VMEM((n_row, VECS, tpd * TILE), F32),
                pltpu.VMEM((n_row, VECS, tpd * TILE), F32),
                pltpu.VMEM((tpd * TILE, LANES), F32),
                dma((5,)),
                dma((n_row,)), dma((n_row,)), dma((n_col,)), dma((n_col,)),
                dma((n_col,)), dma((n_col,)), dma((n_row,)), dma((n_row,)),
            ],
            compiler_params=pltpu.CompilerParams(
                collective_id=0, has_side_effects=True, vmem_limit_bytes=48 * 1024 * 1024
            ),
        )(
            tile_count, tile_rows.reshape(1, slots), tile_cols.reshape(1, slots), x, ham_tiles
        )
        return out.reshape(packed, tpd, LANES).transpose(1, 0, 2).reshape(tpd, size)

    placed = (
        P(("row", "col"), None),
        P(("row", "col"), None),
        P(("row", "col")),
        P(("row", "col")),
        P(("row", "col")),
    )
    return jax.shard_map(
        shards, mesh=mesh, in_specs=placed, out_specs=P(("row", "col"), None), check_vma=False
    )
```

```python
import functools

import jax
import jax.numpy as jnp
from jax import lax
from jax.experimental import pallas as pl
from jax.experimental.pallas import tpu as pltpu
from jax.sharding import PartitionSpec as P

TILE = 64
VECS = 64
LANES = 128
MESH = pl.DeviceIdType.MESH
F32 = jnp.float32
BF16 = jnp.bfloat16


def parts(value):
    high = value.astype(BF16)
    low = (value - high.astype(F32)).astype(BF16)
    return high, low


def kernel(
    n_row, n_col, tpd, slots,
    count_ref, rows_ref, cols_ref, x_ref, ham_ref, out_ref,
    ham, count, rows, cols, placed, m_high, m_low, far, near, stage, weights, near_t,
    up_own, up_got, low_own, low_got, turned,
    local_sems, far_send, far_recv, near_send, near_recv,
    up_send, up_recv, low_send, low_recv,
):
    r, c = lax.axis_index("row"), lax.axis_index("col")
    a_tiles, b_tiles = n_col * tpd, n_row * tpd
    positions = a_tiles * b_tiles
    packed = TILE * VECS // LANES
    wide = tpd * LANES

    def row_peer(k):
        return (lax.rem(r + k, n_row), c)

    def col_peer(k):
        return (r, lax.rem(c + k, n_col))

    get_x = pltpu.make_async_copy(x_ref, far.at[0], local_sems.at[0])
    get_near = pltpu.make_async_copy(x_ref, near.at[0], local_sems.at[1])
    get_rows = pltpu.make_async_copy(rows_ref, rows, local_sems.at[2])
    get_cols = pltpu.make_async_copy(cols_ref, cols, local_sems.at[3])
    get_count = pltpu.make_async_copy(count_ref, count, local_sems.at[4])
    get_ham = pltpu.make_async_copy(ham_ref, ham, local_sems.at[5])
    for copy in (get_x, get_near, get_ham, get_rows, get_cols, get_count):
        copy.start()

    barrier = pltpu.get_barrier_semaphore()
    for k in range(1, n_row):
        pl.semaphore_signal(barrier, inc=1, device_id=row_peer(k), device_id_type=MESH)
    for k in range(1, n_col):
        pl.semaphore_signal(barrier, inc=1, device_id=col_peer(k), device_id_type=MESH)
    pl.semaphore_wait(barrier, n_row + n_col - 2)

    get_x.wait()
    near_copies = []
    for k in range(1, n_col):
        copy = pltpu.make_async_remote_copy(
            src_ref=far.at[0], dst_ref=near.at[k],
            send_sem=near_send.at[k], recv_sem=near_recv.at[k],
            device_id=col_peer(n_col - k), device_id_type=MESH,
        )
        copy.start()
        near_copies.append(copy)
    far_copies = []
    for k in range(1, n_row):
        copy = pltpu.make_async_remote_copy(
            src_ref=far.at[0], dst_ref=far.at[k],
            send_sem=far_send.at[k], recv_sem=far_recv.at[k],
            device_id=row_peer(n_row - k), device_id_type=MESH,
        )
        copy.start()
        far_copies.append(copy)

    get_rows.wait()
    get_cols.wait()
    get_count.wait()
    at_row = rows[...] - c * tpd
    at_row = jnp.where(at_row < 0, at_row + a_tiles, at_row)
    at_col = cols[...] - r * tpd
    at_col = jnp.where(at_col < 0, at_col + b_tiles, at_col)
    slot = lax.broadcasted_iota(jnp.int32, (1, slots), 1)
    place = jnp.where(slot < count[...], at_row * b_tiles + at_col, -1)
    place = jnp.concatenate([place, place], axis=1)
    spot = lax.broadcasted_iota(jnp.int32, (positions, 2 * slots), 0)
    picks = jnp.where(spot == place, 1.0, 0.0).astype(BF16)

    get_ham.wait()
    for p in range(0, packed, 2):
        high, low = parts(ham[:, p * LANES:(p + 2) * LANES])
        both = jnp.concatenate([high, low], axis=0)
        put = jnp.dot(picks, both, preferred_element_type=F32)
        placed[p * positions:(p + 1) * positions, :] = put[:, :LANES]
        placed[(p + 1) * positions:(p + 2) * positions, :] = put[:, LANES:]

    def unfold(a, carry):
        for b in range(b_tiles):
            tile = placed[pl.ds(a * b_tiles + b, packed, stride=positions), :]
            high, low = parts(tile)
            at = pl.ds(pl.multiple_of(a * packed, packed), packed)
            m_high[at, b * LANES:(b + 1) * LANES] = high
            m_low[at, b * LANES:(b + 1) * LANES] = low
        return carry

    lax.fori_loop(0, a_tiles, unfold, 0)

    lane = lax.broadcasted_iota(jnp.int32, (TILE, LANES), 1)
    left = lane < TILE

    get_near.wait()
    for k in range(n_col):
        if k:
            near_copies[k - 1].wait_recv()
        for t in range(tpd):
            near_t[(k * tpd + t) * packed:(k * tpd + t + 1) * packed, :] = near[
                k, pl.ds(t, packed, stride=tpd), :
            ]
    high, low = parts(near_t[...].T)
    x_both = jnp.concatenate([high, low], axis=0)
    low_copies = []
    for k in list(range(1, n_row)) + [0]:
        block = slice(k * wide, (k + 1) * wide)
        first = jnp.dot(x_both, m_high[:, block], preferred_element_type=F32)
        second = jnp.dot(high, m_low[:, block], preferred_element_type=F32)
        total = first[:LANES] + first[LANES:] + second
        for t in range(0, tpd, 2):
            even = total[:, t * LANES:(t + 1) * LANES]
            odd = total[:, (t + 1) * LANES:(t + 2) * LANES]
            one = even[:TILE] + pltpu.roll(even[TILE:], TILE, 1)
            two = pltpu.roll(odd[:TILE], TILE, 1) + odd[TILE:]
            low_own[k, :, t * TILE:(t + 2) * TILE] = jnp.where(left, one, two)
        if k:
            copy = pltpu.make_async_remote_copy(
                src_ref=low_own.at[k], dst_ref=low_got.at[k],
                send_sem=low_send.at[k], recv_sem=low_recv.at[k],
                device_id=row_peer(k), device_id_type=MESH,
            )
            copy.start()
            low_copies.append(copy)

    half = left[:packed]
    for k in range(n_row):
        if k:
            far_copies[k - 1].wait_recv()
        for t in range(tpd):
            x = far[k, pl.ds(t, packed, stride=tpd), :]
            swapped = pltpu.roll(x, TILE, 1)
            stage[pl.ds(0, packed, stride=2), :] = jnp.where(half, x, 0.0)
            stage[pl.ds(1, packed, stride=2), :] = jnp.where(half, swapped, 0.0)
            stage[pl.ds(TILE, packed, stride=2), :] = jnp.where(half, 0.0, swapped)
            stage[pl.ds(TILE + 1, packed, stride=2), :] = jnp.where(half, 0.0, x)
            high, low = parts(stage[...])
            at = slice((k * tpd + t) * LANES, (k * tpd + t + 1) * LANES)
            weights[at, :LANES] = high
            weights[at, LANES:] = low
    first = jnp.dot(m_high[...], weights[...], preferred_element_type=F32)
    second = jnp.dot(m_low[...], weights[:, :LANES], preferred_element_type=F32)
    up_own[...] = first[:, :LANES] + first[:, LANES:] + second
    up_copies = []
    height = tpd * packed
    for k in range(1, n_col):
        copy = pltpu.make_async_remote_copy(
            src_ref=up_own.at[pl.ds(k * height, height)], dst_ref=up_got.at[k],
            send_sem=up_send.at[k], recv_sem=up_recv.at[k],
            device_id=col_peer(k), device_id_type=MESH,
        )
        copy.start()
        up_copies.append(copy)

    lower = low_own[0]
    for k in range(1, n_row):
        low_copies[k - 1].wait_recv()
        lower += low_got[k]
    turned[...] = jnp.concatenate([lower, lower], axis=0).T
    upper = up_own[:height, :]
    for k in range(1, n_col):
        up_copies[k - 1].wait_recv()
        upper += up_got[k]
    for t in range(tpd):
        even = turned[pl.ds(t * TILE, packed, stride=2), :]
        odd = turned[pl.ds(t * TILE + 1, packed, stride=2), :]
        out_ref[pl.ds(t, packed, stride=tpd), :] = (
            upper[t * packed:(t + 1) * packed] + jnp.where(half, even, odd)
        )
    for copy in near_copies + far_copies + low_copies + up_copies:
        copy.wait_send()


def solution(mesh):
    n_row, n_col = mesh.shape["row"], mesh.shape["col"]

    def shards(x_tiles, ham_tiles, tile_rows, tile_cols, tile_count):
        tpd, size = x_tiles.shape
        slots = ham_tiles.shape[0]
        packed = size // LANES
        a_tiles, b_tiles = n_col * tpd, n_row * tpd
        height = tpd * packed
        x = x_tiles.reshape(tpd, packed, LANES).transpose(1, 0, 2).reshape(height, LANES)
        outside = pl.BlockSpec(memory_space=pltpu.HBM)
        dma = pltpu.SemaphoreType.DMA
        out = pl.pallas_call(
            functools.partial(kernel, n_row, n_col, tpd, slots),
            out_shape=jax.ShapeDtypeStruct((height, LANES), F32),
            in_specs=[outside] * 5,
            out_specs=pl.BlockSpec(memory_space=pltpu.VMEM),
            scratch_shapes=[
                pltpu.VMEM((slots, size), F32),
                pltpu.VMEM((1, 1), jnp.int32),
                pltpu.VMEM((1, slots), jnp.int32),
                pltpu.VMEM((1, slots), jnp.int32),
                pltpu.VMEM((packed * a_tiles * b_tiles, LANES), F32),
                pltpu.VMEM((a_tiles * packed, b_tiles * LANES), BF16),
                pltpu.VMEM((a_tiles * packed, b_tiles * LANES), BF16),
                pltpu.VMEM((n_row, height, LANES), F32),
                pltpu.VMEM((n_col, height, LANES), F32),
                pltpu.VMEM((LANES, LANES), F32),
                pltpu.VMEM((b_tiles * LANES, 2 * LANES), BF16),
                pltpu.VMEM((a_tiles * packed, LANES), F32),
                pltpu.VMEM((a_tiles * packed, LANES), F32),
                pltpu.VMEM((n_col, height, LANES), F32),
                pltpu.VMEM((n_row, VECS, tpd * TILE), F32),
                pltpu.VMEM((n_row, VECS, tpd * TILE), F32),
                pltpu.VMEM((tpd * TILE, LANES), F32),
                dma((6,)),
                dma((n_row,)), dma((n_row,)), dma((n_col,)), dma((n_col,)),
                dma((n_col,)), dma((n_col,)), dma((n_row,)), dma((n_row,)),
            ],
            compiler_params=pltpu.CompilerParams(
                collective_id=0, has_side_effects=True, vmem_limit_bytes=60 * 1024 * 1024
            ),
        )(
            tile_count.reshape(1, 1), tile_rows.reshape(1, slots), tile_cols.reshape(1, slots), x, ham_tiles
        )
        return out.reshape(packed, tpd, LANES).transpose(1, 0, 2).reshape(tpd, size)

    placed = (
        P(("row", "col"), None),
        P(("row", "col"), None),
        P(("row", "col")),
        P(("row", "col")),
        P(("row", "col")),
    )
    return jax.shard_map(
        shards, mesh=mesh, in_specs=placed, out_specs=P(("row", "col"), None), check_vma=False
    )
```

```python
import functools

import jax
import jax.numpy as jnp
from jax import lax
from jax.experimental import pallas as pl
from jax.experimental.pallas import tpu as pltpu
from jax.sharding import PartitionSpec as P

TILE = 64
VECS = 64
LANES = 128
MESH = pl.DeviceIdType.MESH
F32 = jnp.float32
BF16 = jnp.bfloat16


def parts(value):
    high = value.astype(BF16)
    low = (value - high.astype(F32)).astype(BF16)
    return high, low


def kernel(
    n_row, n_col, tpd, slots,
    count_ref, rows_ref, cols_ref, x_ref, ham_ref, out_ref,
    ham, rows, cols, placed, m_high, m_low, far, near, stage, weights, near_t,
    up_own, up_got, low_own, low_got, turned,
    local_sems, far_send, far_recv, near_send, near_recv,
    up_send, up_recv, low_send, low_recv,
):
    r, c = lax.axis_index("row"), lax.axis_index("col")
    a_tiles, b_tiles = n_col * tpd, n_row * tpd
    positions = a_tiles * b_tiles
    packed = TILE * VECS // LANES
    wide = tpd * LANES
    order = sorted(range(1, n_row), key=lambda k: -min(k, n_row - k))

    def row_peer(k):
        return (lax.rem(r + k, n_row), c)

    def col_peer(k):
        return (r, lax.rem(c + k, n_col))

    barrier = pltpu.get_barrier_semaphore()
    for k in range(1, n_row):
        pl.semaphore_signal(barrier, inc=1, device_id=row_peer(k), device_id_type=MESH)
    for k in range(1, n_col):
        pl.semaphore_signal(barrier, inc=1, device_id=col_peer(k), device_id_type=MESH)

    get_x = pltpu.make_async_copy(x_ref, far.at[0], local_sems.at[0])
    get_near = pltpu.make_async_copy(x_ref, near.at[0], local_sems.at[1])
    get_rows = pltpu.make_async_copy(rows_ref, rows, local_sems.at[2])
    get_cols = pltpu.make_async_copy(cols_ref, cols, local_sems.at[3])
    get_ham = pltpu.make_async_copy(ham_ref, ham, local_sems.at[4])
    for copy in (get_x, get_near, get_ham, get_rows, get_cols):
        copy.start()

    pl.semaphore_wait(barrier, n_row + n_col - 2)

    get_x.wait()
    near_copies = []
    for k in range(1, n_col):
        copy = pltpu.make_async_remote_copy(
            src_ref=far.at[0], dst_ref=near.at[k],
            send_sem=near_send.at[k], recv_sem=near_recv.at[k],
            device_id=col_peer(n_col - k), device_id_type=MESH,
        )
        copy.start()
        near_copies.append(copy)
    far_copies = {}
    for k in order:
        copy = pltpu.make_async_remote_copy(
            src_ref=far.at[0], dst_ref=far.at[k],
            send_sem=far_send.at[k], recv_sem=far_recv.at[k],
            device_id=row_peer(n_row - k), device_id_type=MESH,
        )
        copy.start()
        far_copies[k] = copy

    get_rows.wait()
    get_cols.wait()
    at_row = rows[...] - c * tpd
    at_row = jnp.where(at_row < 0, at_row + a_tiles, at_row)
    at_col = cols[...] - r * tpd
    at_col = jnp.where(at_col < 0, at_col + b_tiles, at_col)
    slot = lax.broadcasted_iota(jnp.int32, (1, slots), 1)
    place = jnp.where(slot < count_ref[0], at_row * b_tiles + at_col, -1)
    place = jnp.concatenate([place, place], axis=1)
    spot = lax.broadcasted_iota(jnp.int32, (positions, 2 * slots), 0)
    picks = jnp.where(spot == place, 1.0, 0.0).astype(BF16)

    get_ham.wait()
    for p in range(0, packed, 2):
        high, low = parts(ham[:, p * LANES:(p + 2) * LANES])
        both = jnp.concatenate([high, low], axis=0)
        put = jnp.dot(picks, both, preferred_element_type=F32)
        placed[p * positions:(p + 1) * positions, :] = put[:, :LANES]
        placed[(p + 1) * positions:(p + 2) * positions, :] = put[:, LANES:]

    def unfold(a, carry):
        for b in range(b_tiles):
            tile = placed[pl.ds(a * b_tiles + b, packed, stride=positions), :]
            high, low = parts(tile)
            at = pl.ds(pl.multiple_of(a * packed, packed), packed)
            m_high[at, b * LANES:(b + 1) * LANES] = high
            m_low[at, b * LANES:(b + 1) * LANES] = low
        return carry

    lax.fori_loop(0, a_tiles, unfold, 0)

    lane = lax.broadcasted_iota(jnp.int32, (TILE, LANES), 1)
    left = lane < TILE

    half = left[:packed]
    for k in range(n_row):
        if k:
            far_copies[k].wait_recv()
        for t in range(tpd):
            x = far[k, pl.ds(t, packed, stride=tpd), :]
            swapped = pltpu.roll(x, TILE, 1)
            stage[pl.ds(0, packed, stride=2), :] = jnp.where(half, x, 0.0)
            stage[pl.ds(1, packed, stride=2), :] = jnp.where(half, swapped, 0.0)
            stage[pl.ds(TILE, packed, stride=2), :] = jnp.where(half, 0.0, swapped)
            stage[pl.ds(TILE + 1, packed, stride=2), :] = jnp.where(half, 0.0, x)
            high, low = parts(stage[...])
            at = slice((k * tpd + t) * LANES, (k * tpd + t + 1) * LANES)
            weights[at, :LANES] = high
            weights[at, LANES:] = low
    first = jnp.dot(m_high[...], weights[...], preferred_element_type=F32)
    second = jnp.dot(m_low[...], weights[:, :LANES], preferred_element_type=F32)
    up_own[...] = first[:, :LANES] + first[:, LANES:] + second
    up_copies = []
    height = tpd * packed
    for k in range(1, n_col):
        copy = pltpu.make_async_remote_copy(
            src_ref=up_own.at[pl.ds(k * height, height)], dst_ref=up_got.at[k],
            send_sem=up_send.at[k], recv_sem=up_recv.at[k],
            device_id=col_peer(k), device_id_type=MESH,
        )
        copy.start()
        up_copies.append(copy)

    get_near.wait()
    for k in range(n_col):
        if k:
            near_copies[k - 1].wait_recv()
        for t in range(tpd):
            near_t[(k * tpd + t) * packed:(k * tpd + t + 1) * packed, :] = near[
                k, pl.ds(t, packed, stride=tpd), :
            ]
    high, low = parts(near_t[...].T)
    x_both = jnp.concatenate([high, low], axis=0)
    low_copies = {}
    for k in order + [0]:
        block = slice(k * wide, (k + 1) * wide)
        first = jnp.dot(x_both, m_high[:, block], preferred_element_type=F32)
        second = jnp.dot(high, m_low[:, block], preferred_element_type=F32)
        total = first[:LANES] + first[LANES:] + second
        for t in range(0, tpd, 2):
            even = total[:, t * LANES:(t + 1) * LANES]
            odd = total[:, (t + 1) * LANES:(t + 2) * LANES]
            one = even[:TILE] + pltpu.roll(even[TILE:], TILE, 1)
            two = pltpu.roll(odd[:TILE], TILE, 1) + odd[TILE:]
            low_own[k, :, t * TILE:(t + 2) * TILE] = jnp.where(left, one, two)
        if k:
            copy = pltpu.make_async_remote_copy(
                src_ref=low_own.at[k], dst_ref=low_got.at[k],
                send_sem=low_send.at[k], recv_sem=low_recv.at[k],
                device_id=row_peer(k), device_id_type=MESH,
            )
            copy.start()
            low_copies[k] = copy

    lower = low_own[0]
    for k in range(1, n_row):
        low_copies[k].wait_recv()
        lower += low_got[k]
    turned[...] = jnp.concatenate([lower, lower], axis=0).T
    upper = up_own[:height, :]
    for k in range(1, n_col):
        up_copies[k - 1].wait_recv()
        upper += up_got[k]
    for t in range(tpd):
        even = turned[pl.ds(t * TILE, packed, stride=2), :]
        odd = turned[pl.ds(t * TILE + 1, packed, stride=2), :]
        out_ref[pl.ds(t, packed, stride=tpd), :] = (
            upper[t * packed:(t + 1) * packed] + jnp.where(half, even, odd)
        )
    for copy in near_copies + up_copies + list(far_copies.values()) + list(low_copies.values()):
        copy.wait_send()


def solution(mesh):
    n_row, n_col = mesh.shape["row"], mesh.shape["col"]

    def shards(x_tiles, ham_tiles, tile_rows, tile_cols, tile_count):
        tpd, size = x_tiles.shape
        slots = ham_tiles.shape[0]
        packed = size // LANES
        a_tiles, b_tiles = n_col * tpd, n_row * tpd
        height = tpd * packed
        x = x_tiles.reshape(tpd, packed, LANES).transpose(1, 0, 2).reshape(height, LANES)
        outside = pl.BlockSpec(memory_space=pltpu.HBM)
        dma = pltpu.SemaphoreType.DMA
        out = pl.pallas_call(
            functools.partial(kernel, n_row, n_col, tpd, slots),
            out_shape=pltpu.VMEM((height, LANES), F32),
            in_specs=[pl.BlockSpec(memory_space=pltpu.SMEM)] + [outside] * 4,
            out_specs=pl.BlockSpec(memory_space=pltpu.VMEM),
            scratch_shapes=[
                pltpu.VMEM((slots, size), F32),
                pltpu.VMEM((1, slots), jnp.int32),
                pltpu.VMEM((1, slots), jnp.int32),
                pltpu.VMEM((packed * a_tiles * b_tiles, LANES), F32),
                pltpu.VMEM((a_tiles * packed, b_tiles * LANES), BF16),
                pltpu.VMEM((a_tiles * packed, b_tiles * LANES), BF16),
                pltpu.VMEM((n_row, height, LANES), F32),
                pltpu.VMEM((n_col, height, LANES), F32),
                pltpu.VMEM((LANES, LANES), F32),
                pltpu.VMEM((b_tiles * LANES, 2 * LANES), BF16),
                pltpu.VMEM((a_tiles * packed, LANES), F32),
                pltpu.VMEM((a_tiles * packed, LANES), F32),
                pltpu.VMEM((n_col, height, LANES), F32),
                pltpu.VMEM((n_row, VECS, tpd * TILE), F32),
                pltpu.VMEM((n_row, VECS, tpd * TILE), F32),
                pltpu.VMEM((tpd * TILE, LANES), F32),
                dma((5,)),
                dma((n_row,)), dma((n_row,)), dma((n_col,)), dma((n_col,)),
                dma((n_col,)), dma((n_col,)), dma((n_row,)), dma((n_row,)),
            ],
            compiler_params=pltpu.CompilerParams(
                collective_id=0, has_side_effects=True, vmem_limit_bytes=60 * 1024 * 1024
            ),
        )(
            tile_count, tile_rows.reshape(1, slots), tile_cols.reshape(1, slots), x, ham_tiles
        )
        return out.reshape(packed, tpd, LANES).transpose(1, 0, 2).reshape(tpd, size)

    placed = (
        P(("row", "col"), None),
        P(("row", "col"), None),
        P(("row", "col")),
        P(("row", "col")),
        P(("row", "col")),
    )
    return jax.shard_map(
        shards, mesh=mesh, in_specs=placed, out_specs=P(("row", "col"), None), check_vma=False
    )
```

```python
import functools

import jax
import jax.numpy as jnp
from jax import lax
from jax.experimental import pallas as pl
from jax.experimental.pallas import tpu as pltpu
from jax.sharding import PartitionSpec as P

TILE = 64
VECS = 64
LANES = 128
MESH = pl.DeviceIdType.MESH
F32 = jnp.float32
BF16 = jnp.bfloat16


def parts(value):
    high = value.astype(BF16)
    low = (value - high.astype(F32)).astype(BF16)
    return high, low


def kernel(
    n_row, n_col, tpd, slots,
    count_ref, rows_ref, cols_ref, x_ref, ham_ref, out_ref,
    ham, rows, cols, placed, m_high, m_low, far, near, stage, weights, near_t,
    up_own, up_got, low_own, low_got, turned,
    local_sems, far_send, far_recv, near_send, near_recv,
    up_send, up_recv, low_send, low_recv,
):
    r, c = lax.axis_index("row"), lax.axis_index("col")
    a_tiles, b_tiles = n_col * tpd, n_row * tpd
    positions = a_tiles * b_tiles
    packed = TILE * VECS // LANES
    wide = tpd * LANES
    order = sorted(range(1, n_row), key=lambda k: -min(k, n_row - k))

    def row_peer(k):
        return (lax.rem(r + k, n_row), c)

    def col_peer(k):
        return (r, lax.rem(c + k, n_col))

    barrier = pltpu.get_barrier_semaphore()
    for k in range(1, n_row):
        pl.semaphore_signal(barrier, inc=1, device_id=row_peer(k), device_id_type=MESH)
    for k in range(1, n_col):
        pl.semaphore_signal(barrier, inc=1, device_id=col_peer(k), device_id_type=MESH)

    get_x = pltpu.make_async_copy(x_ref, far.at[0], local_sems.at[0])
    get_near = pltpu.make_async_copy(x_ref, near.at[0], local_sems.at[1])
    get_rows = pltpu.make_async_copy(rows_ref, rows, local_sems.at[2])
    get_cols = pltpu.make_async_copy(cols_ref, cols, local_sems.at[3])
    get_ham = pltpu.make_async_copy(ham_ref, ham, local_sems.at[4])
    for copy in (get_x, get_near, get_ham, get_rows, get_cols):
        copy.start()

    pl.semaphore_wait(barrier, n_row + n_col - 2)

    get_x.wait()
    near_copies = []
    for k in range(1, n_col):
        copy = pltpu.make_async_remote_copy(
            src_ref=far.at[0], dst_ref=near.at[k],
            send_sem=near_send.at[k], recv_sem=near_recv.at[k],
            device_id=col_peer(n_col - k), device_id_type=MESH,
        )
        copy.start()
        near_copies.append(copy)
    far_copies = {}
    for k in order:
        copy = pltpu.make_async_remote_copy(
            src_ref=far.at[0], dst_ref=far.at[k],
            send_sem=far_send.at[k], recv_sem=far_recv.at[k],
            device_id=row_peer(n_row - k), device_id_type=MESH,
        )
        copy.start()
        far_copies[k] = copy

    get_rows.wait()
    get_cols.wait()
    at_row = rows[...] - c * tpd
    at_row = jnp.where(at_row < 0, at_row + a_tiles, at_row)
    at_col = cols[...] - r * tpd
    at_col = jnp.where(at_col < 0, at_col + b_tiles, at_col)
    slot = lax.broadcasted_iota(jnp.int32, (1, slots), 1)
    place = jnp.where(slot < count_ref[0], at_row * b_tiles + at_col, -1)
    place = jnp.concatenate([place, place], axis=1)
    spot = lax.broadcasted_iota(jnp.int32, (positions, 2 * slots), 0)
    picks = jnp.where(spot == place, 1.0, 0.0).astype(BF16)

    get_ham.wait()
    for p in range(0, packed, 2):
        high, low = parts(ham[:, p * LANES:(p + 2) * LANES])
        both = jnp.concatenate([high, low], axis=0)
        put = jnp.dot(picks, both, preferred_element_type=F32)
        placed[p * positions:(p + 1) * positions, :] = put[:, :LANES]
        placed[(p + 1) * positions:(p + 2) * positions, :] = put[:, LANES:]

    def unfold(a, carry):
        for b in range(b_tiles):
            tile = placed[pl.ds(a * b_tiles + b, packed, stride=positions), :]
            high, low = parts(tile)
            at = pl.ds(pl.multiple_of(a * packed, packed), packed)
            m_high[at, b * LANES:(b + 1) * LANES] = high
            m_low[at, b * LANES:(b + 1) * LANES] = low
        return carry

    lax.fori_loop(0, a_tiles, unfold, 0)

    lane = lax.broadcasted_iota(jnp.int32, (TILE, LANES), 1)
    left = lane < TILE

    half = left[:packed]
    for k in [0] + order[::-1]:
        if k:
            far_copies[k].wait_recv()
        for t in range(tpd):
            x = far[k, pl.ds(t, packed, stride=tpd), :]
            swapped = pltpu.roll(x, TILE, 1)
            stage[pl.ds(0, packed, stride=2), :] = jnp.where(half, x, 0.0)
            stage[pl.ds(1, packed, stride=2), :] = jnp.where(half, swapped, 0.0)
            stage[pl.ds(TILE, packed, stride=2), :] = jnp.where(half, 0.0, swapped)
            stage[pl.ds(TILE + 1, packed, stride=2), :] = jnp.where(half, 0.0, x)
            high, low = parts(stage[...])
            at = slice((k * tpd + t) * LANES, (k * tpd + t + 1) * LANES)
            weights[at, :LANES] = high
            weights[at, LANES:] = low
    height = tpd * packed
    first = jnp.dot(m_high[height:, :], weights[...], preferred_element_type=F32)
    second = jnp.dot(m_low[height:, :], weights[:, :LANES], preferred_element_type=F32)
    up_own[height:, :] = first[:, :LANES] + first[:, LANES:] + second
    up_copies = []
    for k in range(1, n_col):
        copy = pltpu.make_async_remote_copy(
            src_ref=up_own.at[pl.ds(k * height, height)], dst_ref=up_got.at[k],
            send_sem=up_send.at[k], recv_sem=up_recv.at[k],
            device_id=col_peer(k), device_id_type=MESH,
        )
        copy.start()
        up_copies.append(copy)

    get_near.wait()
    for k in range(n_col):
        if k:
            near_copies[k - 1].wait_recv()
        for t in range(tpd):
            near_t[(k * tpd + t) * packed:(k * tpd + t + 1) * packed, :] = near[
                k, pl.ds(t, packed, stride=tpd), :
            ]
    high, low = parts(near_t[...].T)
    x_both = jnp.concatenate([high, low], axis=0)
    low_copies = {}
    for k in order + [0]:
        block = slice(k * wide, (k + 1) * wide)
        first = jnp.dot(x_both, m_high[:, block], preferred_element_type=F32)
        second = jnp.dot(high, m_low[:, block], preferred_element_type=F32)
        total = first[:LANES] + first[LANES:] + second
        for t in range(0, tpd, 2):
            even = total[:, t * LANES:(t + 1) * LANES]
            odd = total[:, (t + 1) * LANES:(t + 2) * LANES]
            one = even[:TILE] + pltpu.roll(even[TILE:], TILE, 1)
            two = pltpu.roll(odd[:TILE], TILE, 1) + odd[TILE:]
            low_own[k, :, t * TILE:(t + 2) * TILE] = jnp.where(left, one, two)
        if k:
            copy = pltpu.make_async_remote_copy(
                src_ref=low_own.at[k], dst_ref=low_got.at[k],
                send_sem=low_send.at[k], recv_sem=low_recv.at[k],
                device_id=row_peer(k), device_id_type=MESH,
            )
            copy.start()
            low_copies[k] = copy

    first = jnp.dot(m_high[:height, :], weights[...], preferred_element_type=F32)
    second = jnp.dot(m_low[:height, :], weights[:, :LANES], preferred_element_type=F32)
    up_own[:height, :] = first[:, :LANES] + first[:, LANES:] + second

    upper = up_own[:height, :]
    for k in range(1, n_col):
        up_copies[k - 1].wait_recv()
        upper += up_got[k]
    lower = low_own[0]
    for k in range(1, n_row):
        low_copies[k].wait_recv()
        lower += low_got[k]
    turned[...] = jnp.concatenate([lower, lower], axis=0).T
    for t in range(tpd):
        even = turned[pl.ds(t * TILE, packed, stride=2), :]
        odd = turned[pl.ds(t * TILE + 1, packed, stride=2), :]
        out_ref[pl.ds(t, packed, stride=tpd), :] = (
            upper[t * packed:(t + 1) * packed] + jnp.where(half, even, odd)
        )
    for copy in near_copies + up_copies + list(far_copies.values()) + list(low_copies.values()):
        copy.wait_send()


def solution(mesh):
    n_row, n_col = mesh.shape["row"], mesh.shape["col"]

    def shards(x_tiles, ham_tiles, tile_rows, tile_cols, tile_count):
        tpd, size = x_tiles.shape
        slots = ham_tiles.shape[0]
        packed = size // LANES
        a_tiles, b_tiles = n_col * tpd, n_row * tpd
        height = tpd * packed
        x = x_tiles.reshape(tpd, packed, LANES).transpose(1, 0, 2).reshape(height, LANES)
        outside = pl.BlockSpec(memory_space=pltpu.HBM)
        dma = pltpu.SemaphoreType.DMA
        out = pl.pallas_call(
            functools.partial(kernel, n_row, n_col, tpd, slots),
            out_shape=pltpu.VMEM((height, LANES), F32),
            in_specs=[pl.BlockSpec(memory_space=pltpu.SMEM)] + [outside] * 4,
            out_specs=pl.BlockSpec(memory_space=pltpu.VMEM),
            scratch_shapes=[
                pltpu.VMEM((slots, size), F32),
                pltpu.VMEM((1, slots), jnp.int32),
                pltpu.VMEM((1, slots), jnp.int32),
                pltpu.VMEM((packed * a_tiles * b_tiles, LANES), F32),
                pltpu.VMEM((a_tiles * packed, b_tiles * LANES), BF16),
                pltpu.VMEM((a_tiles * packed, b_tiles * LANES), BF16),
                pltpu.VMEM((n_row, height, LANES), F32),
                pltpu.VMEM((n_col, height, LANES), F32),
                pltpu.VMEM((LANES, LANES), F32),
                pltpu.VMEM((b_tiles * LANES, 2 * LANES), BF16),
                pltpu.VMEM((a_tiles * packed, LANES), F32),
                pltpu.VMEM((a_tiles * packed, LANES), F32),
                pltpu.VMEM((n_col, height, LANES), F32),
                pltpu.VMEM((n_row, VECS, tpd * TILE), F32),
                pltpu.VMEM((n_row, VECS, tpd * TILE), F32),
                pltpu.VMEM((tpd * TILE, LANES), F32),
                dma((5,)),
                dma((n_row,)), dma((n_row,)), dma((n_col,)), dma((n_col,)),
                dma((n_col,)), dma((n_col,)), dma((n_row,)), dma((n_row,)),
            ],
            compiler_params=pltpu.CompilerParams(
                collective_id=0, has_side_effects=True, vmem_limit_bytes=60 * 1024 * 1024
            ),
        )(
            tile_count, tile_rows.reshape(1, slots), tile_cols.reshape(1, slots), x, ham_tiles
        )
        return out.reshape(packed, tpd, LANES).transpose(1, 0, 2).reshape(tpd, size)

    placed = (
        P(("row", "col"), None),
        P(("row", "col"), None),
        P(("row", "col")),
        P(("row", "col")),
        P(("row", "col")),
    )
    return jax.shard_map(
        shards, mesh=mesh, in_specs=placed, out_specs=P(("row", "col"), None), check_vma=False
    )
```
